256 devices in a mesh: pair: 8 (over x, core), section: 32 (over z, y).
Axes of the slice: x: 4, y: 4, z: 8, core: 2. Of those that a mesh axis runs over, the one named last changes fastest.
Arguments:
- queries: bfloat16 [8, 4096, 4096], P('pair', 'section'), may hold values from -160 to 160
- keys: bfloat16 [8, 4096, 512], P('pair', 'section'), may hold values from -6 to 6
- values: bfloat16 [8, 4096, 512], P('pair', 'section'), may hold values from -6 to 6
- prefix_keys: bfloat16 [256, 512], P('section'), may hold values from -6 to 6
- prefix_values: bfloat16 [256, 512], P('section'), may hold values from -6 to 6
- lengths: int32 [8], replicated, may hold values from 512 to 4096, as said below
- partner: int32 [8], replicated, may hold values from 0 to 7, as said below
Outputs:
- first_order: bfloat16 [8, 4096, 4096], P('pair', 'section')
- second_order: bfloat16 [8, 4096, 4096], P('pair', 'section')
The draws below stay inside these ranges and needn't reach their ends.
Inputs may be any that keep to these rules, and one draw needn't show every extreme that they name: `lengths`: one response has exactly 4096 tokens. partner[r] = r xor m for one m from 1 to 7 common to the whole list, so partner[partner[r]] = r.
All inputs are finite; a program needn't handle non-finite values.
Results may differ from the reference program's by a relative error of at most 0.018.
Values may be sent and summed in bfloat16 or wider, within the bound.
A program may use at most 128 MiB of HBM per device.

```python
import math
import jax
import jax.numpy as jnp
from jax import lax

QH = 32
KVH = 4
DH = 128
R = 8
LEN = 4096
PRE = 256


def shared_draw(key):
    base_keys = jnp.clip(jax.random.normal(jax.random.fold_in(key, 901), (R, LEN, KVH * DH), jnp.float32), -5.0, 5.0)
    return base_keys


def draw_keys(key, part):
    base_keys = shared_draw(key)
    result = base_keys
    return result.astype(jnp.bfloat16)


def draw_queries(key, part):
    key = jax.random.fold_in(key, 2)
    result = jnp.clip(jax.random.normal(key, (R, LEN, QH * DH), jnp.float32), -5.0, 5.0)
    return result.astype(jnp.bfloat16)


def draw_lengths(key, part):
    key = jax.random.fold_in(key, 3)
    drawn_lengths = jax.random.randint(key, (R,), LEN // 8, LEN + 1)
    longest = jax.random.randint(jax.random.fold_in(key, 4), (), 0, R)
    return jnp.where(jnp.arange(R) == longest, LEN, drawn_lengths).astype(jnp.int32)


def draw_partner(key, part):
    key = jax.random.fold_in(key, 17)
    raw_bits = jax.random.bits(key, (), jnp.uint32)
    distance = (raw_bits % jnp.uint32(R - 1)).astype(jnp.int32) + 1
    return jnp.bitwise_xor(jnp.arange(R, dtype=jnp.int32), distance)


def block_scale(stream_key, shape, shards, low, largest):
    def one(dim, blocks):
        steps = jax.random.uniform(jax.random.fold_in(jax.random.fold_in(stream_key, 6), dim), (blocks,), jnp.float32, low / len(shards), largest / len(shards))
        return jnp.repeat(jnp.exp(steps), shape[dim] // blocks).reshape((-1,) + (1,) * (len(shape) - dim - 1))

    level = one(*shards[0])
    for cut in shards[1:]:
        level = level * one(*cut)
    return level


def normal_values(rng, extent, width, limit, cuts=(), kind=jnp.bfloat16):
    array = width * jax.random.normal(rng, extent, jnp.float32)
    if cuts:
        array = array * block_scale(rng, extent, cuts, -0.22, 0.18)
    return jnp.clip(array, -limit, limit).astype(kind)


def setup_inputs(seed: int = 0) -> dict:
    streams_of = jax.random.split(jax.random.key(seed), 8)
    queries = draw_queries(jax.random.fold_in(streams_of[7], 71), 0)
    keys = draw_keys(jax.random.fold_in(streams_of[7], 71), 0)
    values = normal_values(streams_of[2], (R, LEN, KVH * DH), 1.0, 6.0, ((0, 8), (1, 32)))
    prefix_keys = normal_values(streams_of[3], (PRE, KVH * DH), 1.0, 6.0, ((0, 32),))
    prefix_values = normal_values(streams_of[4], (PRE, KVH * DH), 1.0, 6.0, ((0, 32),))
    lengths = draw_lengths(jax.random.fold_in(streams_of[7], 71), 0)
    partner = draw_partner(jax.random.fold_in(streams_of[7], 71), 0)
    return dict(queries=queries, keys=keys, values=values, prefix_keys=prefix_keys, prefix_values=prefix_values, lengths=lengths, partner=partner)


NEGATIVE = -1.0e30


def head_scores(query_block, key_block):
    scores = jnp.einsum("qkgd,skd->kgqs", query_block.astype(jnp.float32), key_block.astype(jnp.float32))
    return scores * (DH ** -0.5)


def softmax_mix(scores, allowed, value_block):
    masked = jnp.where(allowed, scores, NEGATIVE)
    row_max = jnp.max(masked, axis=-1, keepdims=True)
    weights = jnp.where(allowed, jnp.exp(masked - row_max), 0.0)
    weight_total = jnp.sum(weights, axis=-1)
    rounded = lax.optimization_barrier(weights.astype(jnp.bfloat16)).astype(jnp.float32)
    mixture = jnp.einsum("kgqs,skd->kgqd", rounded, value_block.astype(jnp.float32))
    return mixture / weight_total[..., None]


def reference(queries, keys, values, prefix_keys, prefix_values, lengths, partner):
    group_size = QH // KVH
    block_rows = math.gcd(LEN, 256)
    prefix_key_heads = prefix_keys.reshape(PRE, KVH, DH)
    prefix_value_heads = prefix_values.reshape(PRE, KVH, DH)
    key_positions = jnp.arange(LEN, dtype=jnp.int32)

    def one_response(response):
        partner_slot = partner[response]
        own_length = lengths[response]
        partner_length = lengths[partner_slot]
        query_heads = queries[response].reshape(LEN, KVH, group_size, DH)
        own_keys = keys[response].reshape(LEN, KVH, DH)
        own_values = values[response].reshape(LEN, KVH, DH)
        partner_keys = keys[partner_slot].reshape(LEN, KVH, DH)
        partner_values = values[partner_slot].reshape(LEN, KVH, DH)

        def one_block(block_index):
            block_start = (block_index * block_rows).astype(jnp.int32)
            query_block = lax.dynamic_slice_in_dim(query_heads, block_start, block_rows, 0)
            query_rows = block_start + jnp.arange(block_rows, dtype=jnp.int32)
            prefix_scores = head_scores(query_block, prefix_key_heads)
            own_scores = head_scores(query_block, own_keys)
            partner_scores = head_scores(query_block, partner_keys)
            prefix_allowed = jnp.ones((block_rows, PRE), dtype=jnp.bool_)
            own_allowed = key_positions[None, :] <= query_rows[:, None]
            partner_allowed = jnp.broadcast_to(key_positions[None, :] < partner_length, (block_rows, LEN))
            first_mix = softmax_mix(
                jnp.concatenate([prefix_scores, own_scores], axis=-1),
                jnp.concatenate([prefix_allowed, own_allowed], axis=1),
                jnp.concatenate([prefix_value_heads, own_values], axis=0))
            second_mix = softmax_mix(
                jnp.concatenate([prefix_scores, own_scores, partner_scores], axis=-1),
                jnp.concatenate([prefix_allowed, own_allowed, partner_allowed], axis=1),
                jnp.concatenate([prefix_value_heads, own_values, partner_values], axis=0))
            valid_rows = query_rows < own_length

            def arrange(mixture):
                flattened = mixture.transpose(2, 0, 1, 3).reshape(block_rows, QH * DH)
                return jnp.where(valid_rows[:, None], flattened, 0.0).astype(jnp.bfloat16)

            return arrange(first_mix), arrange(second_mix)

        first_rows, second_rows = lax.map(one_block, jnp.arange(LEN // block_rows, dtype=jnp.int32))
        return first_rows.reshape(LEN, QH * DH), second_rows.reshape(LEN, QH * DH)

    first_order, second_order = lax.map(one_response, jnp.arange(R, dtype=jnp.int32))
    return first_order, second_order
```

```python
import functools

import jax
import jax.numpy as jnp
from jax import lax
from jax.experimental import pallas as pl
from jax.experimental.pallas import tpu as pltpu
from jax.sharding import PartitionSpec as P

QH = 32
KVH = 4
DH = 128
G = QH // KVH
NY = 4
NZ = 8
ROWS = 128
BLK = NY * ROWS
PRE_ROWS = 8
PIECE = 2 * PRE_ROWS
OWN_ROWS = 2 * BLK + NY * PIECE
HALF = OWN_ROWS // 2
NEGATIVE = -1e30
SCALE2 = DH ** -0.5 * 1.4426950408889634
SAFE = 100.0
NT = (((1,), (1,)), ((), ()))
f32 = jnp.float32
bf16 = jnp.bfloat16
VMEM = pltpu.VMEM


def at_section(z, y):
    return {"section": z * NY + y}


def gather_kernel(distance, q_ref, k_ref, v_ref, pk_ref, pv_ref, qh, own, par, pre,
                  local_sem, a2a_send, a2a_recv, ring_send, ring_recv):
    slot = lax.axis_index("pair")
    section = lax.axis_index("section")
    z = section // NY
    y = section % NY
    up = lax.rem(z + 1, NZ)
    down = lax.rem(z + NZ - 1, NZ)
    other = {"pair": slot ^ distance}

    def zb(step):
        return lax.rem(z + step + NZ, NZ)

    barrier = pltpu.get_barrier_semaphore()
    targets = [at_section(z, lax.rem(y + d, NY)) for d in range(1, NY)]
    targets += [at_section(up, y), at_section(down, y), other]
    for target in targets:
        pl.semaphore_signal(barrier, inc=1, device_id=target, device_id_type=pl.DeviceIdType.MESH)
    pre[...] = jnp.concatenate([pk_ref[...].astype(f32), pv_ref[...].astype(f32)], axis=0).astype(bf16)
    pl.semaphore_wait(barrier, len(targets))

    def heads(ref, width, head):
        return ref.at[:, pl.ds(pl.multiple_of(head * width, 128), width)]

    def places(head):
        return [
            (heads(k_ref, DH, head), own.at[z, pl.ds(y * ROWS, ROWS)]),
            (heads(v_ref, DH, head), own.at[z, pl.ds(BLK + y * ROWS, ROWS)]),
            (heads(pre, DH, head), own.at[z, pl.ds(2 * BLK + y * PIECE, PIECE)]),
            (heads(q_ref, G * DH, head), qh.at[y]),
        ]

    copies = []
    for d in range(1, NY):
        head = lax.rem(y + d, NY)
        for i, (src, dst) in enumerate(places(head)):
            copies.append(pltpu.make_async_remote_copy(
                src_ref=src, dst_ref=dst, send_sem=a2a_send.at[d - 1, i], recv_sem=a2a_recv.at[d - 1, i],
                device_id=at_section(z, head), device_id_type=pl.DeviceIdType.MESH))
    kv_copies = [c for i, c in enumerate(copies) if i % 4 != 3]
    q_copies = [c for i, c in enumerate(copies) if i % 4 == 3]
    locals_ = [pltpu.make_async_copy(src, dst, local_sem.at[i]) for i, (src, dst) in enumerate(places(y))]
    for c in kv_copies:
        c.start()
    for c in locals_:
        c.start()
    for c in q_copies:
        c.start()
    for c in locals_[:3]:
        c.wait()
    for c in kv_copies:
        c.wait_recv()

    ring = {}

    def send(name, src, dst, target):
        index = len(ring)
        copy = pltpu.make_async_remote_copy(
            src_ref=src, dst_ref=dst, send_sem=ring_send.at[index], recv_sem=ring_recv.at[index],
            device_id=target, device_id_type=pl.DeviceIdType.MESH)
        copy.start()
        ring[name] = copy

    to_up = at_section(up, y)
    to_down = at_section(down, y)

    def whole(name, step, target):
        send(name, own.at[zb(step)], own.at[zb(step)], target)

    def cross(name, step):
        part = pl.ds(0, 2 * BLK)
        send(name, own.at[zb(step), part], par.at[zb(step)], other)

    whole("u1", 0, to_up)
    whole("d1", 0, to_down)
    cross("x0", 0)
    ring["u1"].wait_recv()
    whole("u2", -1, to_up)
    cross("x-1", -1)
    ring["d1"].wait_recv()
    whole("d2", 1, to_down)
    cross("x+1", 1)
    ring["u2"].wait_recv()
    whole("u3", -2, to_up)
    cross("x-2", -2)
    ring["d2"].wait_recv()
    whole("d3", 2, to_down)
    cross("x+2", 2)
    ring["u3"].wait_recv()
    low = pl.ds(0, HALF)
    high = pl.ds(HALF, HALF)
    send("u4", own.at[zb(-3), low], own.at[zb(-3), low], to_up)
    ring["d3"].wait_recv()
    send("d4", own.at[zb(3), high], own.at[zb(3), high], to_down)
    ring["x-2"].wait_recv()
    send("pu3", par.at[zb(-2)], par.at[zb(-2)], to_up)
    ring["x+2"].wait_recv()
    send("pd3", par.at[zb(2)], par.at[zb(2)], to_down)
    low = pl.ds(0, BLK)
    high = pl.ds(BLK, BLK)
    ring["pu3"].wait_recv()
    send("pu4", par.at[zb(-3), low], par.at[zb(-3), low], to_up)
    ring["pd3"].wait_recv()
    send("pd4", par.at[zb(3), high], par.at[zb(3), high], to_down)
    for name in ("x0", "x-1", "x+1", "u4", "d4", "pu4", "pd4"):
        ring[name].wait_recv()
    locals_[3].wait()
    for c in q_copies:
        c.wait_recv()
    for c in copies:
        c.wait_send()
    for c in ring.values():
        c.wait_send()


def gather(distance, q, k, v, pk, pv):
    vmem = pl.BlockSpec(memory_space=VMEM)
    return pl.pallas_call(
        functools.partial(gather_kernel, distance),
        out_shape=(
            jax.ShapeDtypeStruct((NY, ROWS, G * DH), bf16),
            jax.ShapeDtypeStruct((NZ, OWN_ROWS, DH), bf16),
            jax.ShapeDtypeStruct((NZ, 2 * BLK, DH), bf16),
        ),
        in_specs=[vmem] * 5,
        out_specs=(vmem,) * 3,
        scratch_shapes=[
            VMEM((PIECE, KVH * DH), bf16),
            pltpu.SemaphoreType.DMA((4,)),
            pltpu.SemaphoreType.DMA((NY - 1, 4)),
            pltpu.SemaphoreType.DMA((NY - 1, 4)),
            pltpu.SemaphoreType.DMA((17,)),
            pltpu.SemaphoreType.DMA((17,)),
        ],
        compiler_params=pltpu.CompilerParams(
            collective_id=distance, has_side_effects=True, vmem_limit_bytes=32 << 20),
        name=f"gather_{distance}",
    )(q, k, v, pk, pv)


def attend_kernel(sc, qh, own, par, first, second, pk, pv, acc, total, top):
    z = sc[0]
    own_length = sc[1]
    partner_length = sc[2]

    def query(g):
        return qh[:, :, pl.ds(pl.multiple_of(g * DH, DH), DH)].reshape(BLK, DH)

    def own_kv(b):
        return own[b, pl.ds(0, BLK)], own[b, pl.ds(BLK, BLK)]

    def par_kv(b):
        return par[b, pl.ds(0, BLK)], par[b, pl.ds(BLK, BLK)]

    def causal():
        row = lax.broadcasted_iota(jnp.int32, (BLK, BLK), 0)
        return lax.broadcasted_iota(jnp.int32, (BLK, BLK), 1) <= row

    def before(limit):
        return lax.broadcasted_iota(jnp.int32, (BLK, BLK), 1) < limit

    full = partner_length // BLK
    rest = partner_length - full * BLK

    def store(ref, g, u):
        row = lax.broadcasted_iota(jnp.int32, (BLK, 1), 0) + z * BLK
        weight = jnp.sum(total[u], axis=1, keepdims=True)
        mixed = jnp.where(row < own_length, acc[u] / weight, 0.0).astype(bf16)
        ref[:, :, pl.ds(pl.multiple_of(g * DH, DH), DH)] = mixed.reshape(NY, ROWS, DH)

    def lanes(p):
        return sum(p[:, i * DH:(i + 1) * DH] for i in range(p.shape[1] // DH))

    def tile(g, parts):
        q = query(g)
        a = None
        t = None
        for keys, values, mask in parts:
            s = lax.dot_general(q, keys, NT, preferred_element_type=f32)
            p = jnp.exp2(s * SCALE2)
            if mask is not None:
                p = jnp.where(mask, p, 0.0)
            one = lanes(p)
            mixed = jnp.dot(p.astype(bf16), values, preferred_element_type=f32)
            a = mixed if a is None else a + mixed
            t = one if t is None else t + one
        return a, t

    def add(g, u, parts):
        a, t = tile(g, parts)
        acc[u] += a
        total[u] += t

    def span(pair, kv, count):
        def go(first_block, blocks):
            for u in range(2):
                add(pair * 2 + u, u, [kv(first_block + i) + (None,) for i in range(blocks)])

        def four(i, carry):
            go(i * 4, 4)
            return carry

        lax.fori_loop(0, count // 4, four, 0)

        @pl.when(lax.rem(count // 2, 2) == 1)
        def _():
            go(count // 4 * 4, 2)

        @pl.when(lax.rem(count, 2) == 1)
        def _():
            go(count - 1, 1)

    def fast():
        def one_pair(pair, carry):
            for u in range(2):
                g = pair * 2 + u
                acc[u], total[u] = tile(g, [(pk[...], pv[...], None), own_kv(z) + (causal(),)])
            span(pair, own_kv, z)
            for u in range(2):
                store(first, pair * 2 + u, u)
            span(pair, par_kv, full)

            @pl.when(rest > 0)
            def _():
                for u in range(2):
                    add(pair * 2 + u, u, [par_kv(full) + (before(rest),)])

            for u in range(2):
                store(second, pair * 2 + u, u)
            return carry

        lax.fori_loop(0, G // 2, one_pair, 0)

    def slow():
        def absorb(g, keys, values, mask):
            s = lax.dot_general(query(g), keys, NT, preferred_element_type=f32)
            if mask is not None:
                s = jnp.where(mask, s, NEGATIVE)
            now = jnp.maximum(top[...], jnp.max(s, axis=1, keepdims=True))
            fade = jnp.exp2((top[...] - now) * SCALE2)
            p = jnp.exp2((s - now[:, :1]) * SCALE2)
            if mask is not None:
                p = jnp.where(mask, p, 0.0)
            top[...] = now
            total[0] = total[0] * fade + lanes(p)
            acc[0] = acc[0] * fade + jnp.dot(p.astype(bf16), values, preferred_element_type=f32)

        def one_head(g, carry):
            top[...] = jnp.full_like(top, NEGATIVE)
            total[0] = jnp.zeros((BLK, DH), f32)
            acc[0] = jnp.zeros((BLK, DH), f32)
            absorb(g, pk[...], pv[...], None)
            absorb(g, *own_kv(z), causal())

            def own_block(b, c):
                absorb(g, *own_kv(b), None)
                return c

            def par_block(b, c):
                absorb(g, *par_kv(b), None)
                return c

            lax.fori_loop(0, z, own_block, 0)
            store(first, g, 0)
            lax.fori_loop(0, full, par_block, 0)

            @pl.when(rest > 0)
            def _():
                absorb(g, *par_kv(full), before(rest))

            store(second, g, 0)
            return carry

        lax.fori_loop(0, G, one_head, 0)

    def norm2(x):
        x = x.astype(f32)
        ones = jnp.ones((DH, DH), bf16)
        return jnp.max(jnp.dot((x * x).astype(bf16), ones, preferred_element_type=f32), axis=0, keepdims=True)

    needed = z * BLK < own_length

    @pl.when(jnp.logical_not(needed))
    def _():
        first[...] = jnp.zeros_like(first)
        second[...] = jnp.zeros_like(second)

    @pl.when(needed)
    def _():
        for b in range(NZ):
            piece = own[b, pl.ds(2 * BLK, NY * PIECE)].astype(f32).reshape(NY, 2, PRE_ROWS, DH)
            rows = pl.ds(b * NY * PRE_ROWS, NY * PRE_ROWS)
            pk[rows] = piece[:, 0].reshape(NY * PRE_ROWS, DH).astype(bf16)
            pv[rows] = piece[:, 1].reshape(NY * PRE_ROWS, DH).astype(bf16)

        q_norm = functools.reduce(jnp.maximum, [norm2(query(g)) for g in range(G)])
        k_norm = norm2(pk[...])
        for b in range(NZ):
            k_norm = jnp.maximum(k_norm, jnp.maximum(norm2(own_kv(b)[0]), norm2(par_kv(b)[0])))
        bound = jnp.max(q_norm) * jnp.max(k_norm)
        safe = bound * (1.02 * SCALE2 * SCALE2) < SAFE * SAFE

        @pl.when(safe)
        def _():
            fast()

        @pl.when(jnp.logical_not(safe))
        def _():
            slow()


def attend(sc, qh, own, par):
    vmem = pl.BlockSpec(memory_space=VMEM)
    out = jax.ShapeDtypeStruct((NY, ROWS, G * DH), bf16)
    return pl.pallas_call(
        attend_kernel,
        out_shape=(out, out),
        in_specs=[pl.BlockSpec(memory_space=pltpu.SMEM), vmem, vmem, vmem],
        out_specs=(vmem, vmem),
        scratch_shapes=[
            VMEM((NZ * NY * PRE_ROWS, DH), bf16),
            VMEM((NZ * NY * PRE_ROWS, DH), bf16),
            VMEM((2, BLK, DH), f32),
            VMEM((2, BLK, DH), f32),
            VMEM((BLK, DH), f32),
        ],
        compiler_params=pltpu.CompilerParams(vmem_limit_bytes=48 << 20),
        name="attend",
    )(sc, qh, own, par)


def scatter_kernel(first, second, out1, out2, local_sem, send_sem, recv_sem):
    section = lax.axis_index("section")
    z = section // NY
    y = section % NY
    barrier = pltpu.get_barrier_semaphore()
    for d in range(1, NY):
        pl.semaphore_signal(barrier, inc=1, device_id=at_section(z, lax.rem(y + d, NY)),
                            device_id_type=pl.DeviceIdType.MESH)
    pl.semaphore_wait(barrier, NY - 1)
    mine = pl.ds(pl.multiple_of(y * G * DH, DH), G * DH)
    copies = []
    for i, (src, dst) in enumerate(((first, out1), (second, out2))):
        for d in range(1, NY):
            to = lax.rem(y + d, NY)
            copies.append(pltpu.make_async_remote_copy(
                src_ref=src.at[to], dst_ref=dst.at[:, mine], send_sem=send_sem.at[i, d - 1],
                recv_sem=recv_sem.at[i, d - 1], device_id=at_section(z, to),
                device_id_type=pl.DeviceIdType.MESH))
        copies.append(pltpu.make_async_copy(src.at[y], dst.at[:, mine], local_sem.at[i]))
    for c in copies:
        c.start()
    for c in copies:
        c.wait()


def scatter(first, second):
    vmem = pl.BlockSpec(memory_space=VMEM)
    out = jax.ShapeDtypeStruct((ROWS, QH * DH), bf16)
    return pl.pallas_call(
        scatter_kernel,
        out_shape=(out, out),
        in_specs=[vmem, vmem],
        out_specs=(vmem, vmem),
        scratch_shapes=[
            pltpu.SemaphoreType.DMA((2,)),
            pltpu.SemaphoreType.DMA((2, NY - 1)),
            pltpu.SemaphoreType.DMA((2, NY - 1)),
        ],
        compiler_params=pltpu.CompilerParams(
            collective_id=8, has_side_effects=True, vmem_limit_bytes=32 << 20),
        name="scatter",
    )(first, second)


def local(queries, keys, values, prefix_keys, prefix_values, lengths, partner):
    slot = lax.axis_index("pair")
    section = lax.axis_index("section")
    partner_slot = partner[slot]
    distance = jnp.bitwise_xor(partner[0], 0)
    branches = [functools.partial(gather, d) for d in range(1, 8)]
    qh, own, par = lax.switch(
        distance - 1, branches, queries[0], keys[0], values[0], prefix_keys, prefix_values)
    sc = jnp.stack([section // NY, lengths[slot], lengths[partner_slot]]).astype(jnp.int32)
    first, second = attend(sc, qh, own, par)
    out1, out2 = scatter(first, second)
    return out1[None], out2[None]


def solution(mesh):
    in_specs = (
        P("pair", "section", None),
        P("pair", "section", None),
        P("pair", "section", None),
        P("section", None),
        P("section", None),
        P(),
        P(),
    )
    out_specs = (P("pair", "section", None), P("pair", "section", None))
    return jax.shard_map(local, mesh=mesh, in_specs=in_specs, out_specs=out_specs, check_vma=False)
```

```python
import functools

import jax
import jax.numpy as jnp
from jax import lax
from jax.experimental import pallas as pl
from jax.experimental.pallas import tpu as pltpu
from jax.sharding import PartitionSpec as P

QH = 32
KVH = 4
DH = 128
G = QH // KVH
NY = 4
NZ = 8
ROWS = 128
BLK = NY * ROWS
PRE_ROWS = 8
PIECE = 2 * PRE_ROWS
OWN_ROWS = 2 * BLK + NY * PIECE + 16
STACK = G * ROWS
SCALE2 = DH ** -0.5 * 1.4426950408889634
SAFE = 100.0
NEGATIVE = -1e30
NT = (((1,), (1,)), ((), ()))
f32 = jnp.float32
bf16 = jnp.bfloat16
VMEM = pltpu.VMEM
MESH = pl.DeviceIdType.MESH

def careful_kernel(sc, q, k, v, first, second, top, weight, mixed):
    block = pl.program_id(1)
    span = k.shape[0]
    prompt, length = PRE_ROWS * NY * NZ, ROWS * NY * NZ
    split = (prompt + length) // span

    @pl.when(block == 0)
    def _():
        top[...] = jnp.full_like(top, NEGATIVE)
        weight[...] = jnp.zeros_like(weight)
        mixed[...] = jnp.zeros_like(mixed)

    place = lax.broadcasted_iota(jnp.int32, (ROWS, span), 1) + (block * span - prompt)
    row = lax.broadcasted_iota(jnp.int32, (ROWS, span), 0) + sc[0] * ROWS
    limit = jnp.where(block < split, row + 1, length + sc[2])
    allowed = place < limit
    s = lax.dot_general(q[...], k[...], NT, preferred_element_type=f32)
    s = jnp.where(allowed, s, NEGATIVE)
    now = jnp.maximum(top[...], jnp.max(s, axis=1, keepdims=True))
    fade = jnp.exp2((top[...] - now) * SCALE2)
    p = jnp.where(allowed, jnp.exp2((s - now[:, :1]) * SCALE2), 0.0)
    top[...] = now
    weight[...] = weight[...] * fade + jnp.sum(p, axis=1, keepdims=True)
    mixed[...] = mixed[...] * fade + jnp.dot(p.astype(bf16), v[...], preferred_element_type=f32)
    place_row = lax.broadcasted_iota(jnp.int32, (ROWS, DH), 0) + sc[0] * ROWS

    def result():
        return jnp.where(place_row < sc[1], mixed[...] / weight[...], 0.0).astype(bf16)

    @pl.when(block == split - 1)
    def _():
        first[...] = result()

    @pl.when(block == split + length // span - 1)
    def _():
        second[...] = result()


def general(queries, keys, values, prefix_keys, prefix_values, lengths, partner):
    slot = lax.axis_index("pair")
    section = lax.axis_index("section")
    mine = jnp.concatenate([prefix_keys, prefix_values, keys[0], values[0]], axis=0)
    pair = lax.all_gather(mine, "pair")
    theirs = lax.dynamic_index_in_dim(pair, partner[slot], 0, keepdims=False)
    every = lax.all_gather(jnp.concatenate([mine, theirs[2 * PRE_ROWS:]], axis=0), "section")

    def stream(which):
        def rows_of(begin, count):
            return every[:, begin:begin + count].reshape(-1, KVH * DH)

        begin = 2 * PRE_ROWS + which * ROWS
        return jnp.concatenate([
            rows_of(which * PRE_ROWS, PRE_ROWS), rows_of(begin, ROWS), rows_of(begin + 2 * ROWS, ROWS)], axis=0)

    span = PRE_ROWS * NY * NZ
    blocks = (span + 2 * ROWS * NY * NZ) // span
    sc = jnp.stack([section, lengths[slot], lengths[partner[slot]]]).astype(jnp.int32)
    head = pl.BlockSpec((ROWS, DH), lambda h, b: (0, h))
    group = pl.BlockSpec((span, DH), lambda h, b: (b, h // G))
    out = jax.ShapeDtypeStruct((ROWS, QH * DH), bf16)
    first, second = pl.pallas_call(
        careful_kernel,
        out_shape=(out, out),
        grid=(QH, blocks),
        in_specs=[pl.BlockSpec(memory_space=pltpu.SMEM), head, group, group],
        out_specs=(head, head),
        scratch_shapes=[VMEM((ROWS, DH), f32)] * 3,
        name="careful",
    )(sc, queries[0], stream(0), stream(1))
    return first[None], second[None]


Q_FIRST = (1, 3)
Q_SECOND = ()
Q_THIRD = (2,)
LOW = 4
PROMPT = 2 * NZ


def at_section(z, y):
    return {"section": z * NY + y}


def fused_kernel(distance, lengths, q_ref, k_ref, v_ref, pk_ref, pv_ref, out1, out2, level,
                 pre, pre_in, q_in, k_in, qh, kvb, acc, tot, st1, st2, flags,
                 local_sem, a2a_send, a2a_recv, ring_send, ring_recv, out_local, out_send, out_recv,
                 flag_send, flag_recv):
    slot = lax.axis_index("pair")
    section = lax.axis_index("section")
    z = section // NY
    y = section % NY
    up = lax.rem(z + 1, NZ)
    down = lax.rem(z + NZ - 1, NZ)
    other = {"pair": slot ^ distance}
    own_length = lengths[slot]
    partner_length = lengths[slot ^ distance]

    def zb(step):
        return lax.rem(z + step + NZ, NZ)

    barrier = pltpu.get_barrier_semaphore()
    targets = [at_section(z, lax.rem(y + d, NY)) for d in range(1, NY)]
    targets += [at_section(t, y) for t in (up, down)]
    targets += [{"pair": slot ^ d} for d in sorted({1, 2, 4, distance})]
    for target in targets:
        pl.semaphore_signal(barrier, inc=1, device_id=target, device_id_type=MESH)
    staged = [pltpu.make_async_copy(src, dst, local_sem.at[4 + i]) for i, (src, dst) in enumerate(
        ((pk_ref, pre_in.at[0]), (pv_ref, pre_in.at[1]), (k_ref, k_in), (q_ref, q_in)))]
    for c in staged:
        c.start()
    staged[0].wait()
    staged[1].wait()
    pre[...] = jnp.concatenate([pre_in[0].astype(f32), pre_in[1].astype(f32)], axis=0).astype(bf16)
    pl.semaphore_wait(barrier, len(targets))

    def heads(ref, width, head):
        return ref.at[:, pl.ds(pl.multiple_of(head * width, 128), width)]

    def places(head):
        return [
            (heads(k_ref, DH, head), kvb.at[z, pl.ds(y * ROWS, ROWS)]),
            (heads(v_ref, DH, head), kvb.at[z, pl.ds(BLK + y * ROWS, ROWS)]),
            (heads(pre, DH, head), kvb.at[z, pl.ds(2 * BLK + y * PIECE, PIECE)]),
            (heads(q_ref, G * DH, head), qh.at[y]),
        ]

    def start_q_first():
        for d in Q_FIRST:
            q_copies[d].start()

    def start_q_second():
        for d in Q_SECOND:
            q_copies[d].start()

    kv_copies = []
    q_copies = {}
    for d in (1, 3, 2):
        head = lax.rem(y + d, NY)
        for i, (src, dst) in enumerate(places(head)):
            copy = pltpu.make_async_remote_copy(
                src_ref=src, dst_ref=dst, send_sem=a2a_send.at[d - 1, i], recv_sem=a2a_recv.at[d - 1, i],
                device_id=at_section(z, head), device_id_type=MESH)
            if i < 3:
                kv_copies.append(copy)
            else:
                q_copies[d] = copy
    locals_ = [pltpu.make_async_copy(src, dst, local_sem.at[i]) for i, (src, dst) in enumerate(places(y))]
    for c in kv_copies:
        c.start()
    for c in locals_:
        c.start()
    start_q_first()

    ring = {}
    keys_part = pl.ds(0, BLK)
    own_values = pl.ds(BLK, OWN_ROWS - BLK)
    par_values = pl.ds(BLK, BLK)
    to_up = at_section(up, y)
    to_down = at_section(down, y)
    routes = []
    for step in range(3):
        for part, rows in (("k", keys_part), ("v", own_values)):
            routes.append((f"u{step + 1}{part}", zb(-step), rows, to_up))
            routes.append((f"d{step + 1}{part}", zb(step), rows, to_down))
    for step in (0, -1, 1, -2, 2):
        for part, rows in (("k", keys_part), ("v", par_values)):
            routes.append((f"x{step}{part}", zb(step), rows, other))
    for part, rows in (("k", keys_part), ("v", par_values)):
        routes.append((f"pu3{part}", NZ + zb(-2), rows, to_up))
        routes.append((f"pd3{part}", NZ + zb(2), rows, to_down))
    routes.append(("u4k", zb(-3), keys_part, to_up))
    routes.append(("d4v", zb(3), own_values, to_down))
    routes.append(("pu4k", NZ + zb(-3), keys_part, to_up))
    routes.append(("pd4v", NZ + zb(3), par_values, to_down))
    for index, (name, block, rows, target) in enumerate(routes):
        to_block = NZ + block if name[0] == "x" else block
        ring[name] = pltpu.make_async_remote_copy(
            src_ref=kvb.at[block, rows], dst_ref=kvb.at[to_block, rows],
            send_sem=ring_send.at[index], recv_sem=ring_recv.at[index],
            device_id=target, device_id_type=MESH)

    def send(*which):
        for name in which:
            ring[name].start()

    def arrived(*which):
        for name in which:
            ring[name].wait_recv()

    rounds = [at_section(z, y ^ 1), at_section(z, y ^ 2),
              {"pair": slot ^ 1}, {"pair": slot ^ 2}, {"pair": slot ^ 4}]

    def flag_copy(r):
        return pltpu.make_async_remote_copy(
            src_ref=flags.at[0, r], dst_ref=flags.at[1, r], send_sem=flag_send.at[r], recv_sem=flag_recv.at[r],
            device_id=rounds[r], device_id_type=MESH)

    def flag_step(r):
        flag_copy(r).wait_recv()
        both = jnp.maximum(flags[0, r], flags[1, r])
        if r + 1 < len(rounds):
            flags[0, r + 1] = both
            flag_copy(r + 1).start()
        else:
            level[...] = both

    def squares(x):
        x = x.astype(f32)
        x = (x * x).astype(bf16)
        sums = jnp.dot(x, jnp.ones((DH, DH), bf16), preferred_element_type=f32)
        return functools.reduce(jnp.maximum, [sums[i:i + 8] for i in range(0, sums.shape[0], 8)])

    def q_head(h, top):
        return jnp.maximum(top, squares(q_in[:, pl.ds(pl.multiple_of(h * DH, DH), DH)]))

    staged[3].wait()
    q_top = lax.fori_loop(0, QH, q_head, jnp.zeros((8, DH), f32))
    staged[2].wait()
    k_top = jnp.zeros((8, DH), f32)
    for h in range(KVH):
        k_top = jnp.maximum(k_top, squares(k_in[:, h * DH:(h + 1) * DH]))
        k_top = jnp.maximum(k_top, squares(pre[:, h * DH:(h + 1) * DH])[:8])
    kvb[z, pl.ds(OWN_ROWS - 16, 16)] = jnp.concatenate([q_top, k_top], axis=0).astype(bf16)

    def clear(i, carry):
        acc[i] = jnp.zeros((STACK, DH), f32)
        tot[i] = jnp.zeros((STACK, DH), f32)
        return carry

    lax.fori_loop(0, 2 * NY, clear, 0)
    spare = jnp.zeros((BLK - NZ * NY * PRE_ROWS, DH), bf16)
    for begin in (NZ * NY * PRE_ROWS, BLK + NZ * NY * PRE_ROWS):
        kvb[PROMPT, pl.ds(begin, BLK - NZ * NY * PRE_ROWS)] = spare
    for c in locals_[:3]:
        c.wait()
    for c in kv_copies:
        c.wait_recv()
    send("u1k", "d1k", "x0k", "u1v", "d1v", "x0v")
    start_q_second()

    locals_[3].wait()

    def kv(b):
        return kvb[b, pl.ds(0, BLK)], kvb[b, pl.ds(BLK, BLK)]

    def lanes(p):
        return sum(p[:, i * DH:(i + 1) * DH] for i in range(p.shape[1] // DH))

    def unit(c, kind, parts):
        q = jnp.concatenate([qh[c, :, pl.ds(g * DH, DH)] for g in range(G)], axis=0)
        a = None
        t = None
        for keys, values, mask in parts:
            s = lax.dot_general(q, keys, NT, preferred_element_type=f32)
            p = jnp.exp2(s * SCALE2)
            if mask is not None:
                p = jnp.where(mask, p.reshape(G, ROWS, p.shape[1]), 0.0).reshape(p.shape)
            one = lanes(p)
            mixed = jnp.dot(p.astype(bf16), values, preferred_element_type=f32)
            a = mixed if a is None else a + mixed
            t = one if t is None else t + one
        acc[kind * NY + c] += a
        tot[kind * NY + c] += t

    def chunk(i):
        return lax.rem(y + (i ^ (i >> 1)), NY)

    def single(c, kind, b, causal):
        row = lax.broadcasted_iota(jnp.int32, (1, ROWS, 1), 1) + (c * ROWS + 1)
        limit = jnp.where(kind == 1, partner_length - b * BLK, jnp.where(b == PROMPT, NZ * NY * PRE_ROWS, BLK))
        limit = jnp.where(causal, row, limit)
        mask = lax.broadcasted_iota(jnp.int32, (1, ROWS, BLK), 2) < limit
        unit(c, kind, [kv(kind * NZ + b) + (mask,)])

    def double(c, kind, blocks):
        parts = []
        for b in blocks:
            limit = jnp.where(kind == 1, partner_length - b * BLK, BLK)
            mask = lax.broadcasted_iota(jnp.int32, (1, 1, BLK), 2) < limit
            parts.append(kv(kind * NZ + b) + (mask,))
        unit(c, kind, parts)

    mine = pl.ds(pl.multiple_of(y * G * DH, DH), G * DH)

    def out_copy(n, i, c):
        st, out = ((st1, out1), (st2, out2))[n]
        return pltpu.make_async_remote_copy(
            src_ref=st.at[c], dst_ref=out.at[0, :, mine], send_sem=out_send.at[n, i], recv_sem=out_recv.at[n, i],
            device_id=at_section(z, c), device_id_type=MESH)

    def out_own(n):
        st, out = ((st1, out1), (st2, out2))[n]
        return pltpu.make_async_copy(st.at[y], out.at[0, :, mine], out_local.at[n])

    def finish(n, i, c, a, t):
        st = (st1, st2)[n]
        row = lax.broadcasted_iota(jnp.int32, (1, ROWS, 1), 1) + (z * BLK + c * ROWS)
        mixed = (a * (1.0 / jnp.sum(t, axis=1, keepdims=True))).reshape(G, ROWS, DH)
        mixed = jnp.where(row < own_length, mixed, 0.0).astype(bf16)
        for g in range(G):
            st[c, :, pl.ds(g * DH, DH)] = mixed[g]

        @pl.when(i < NY - 1)
        def _():
            out_copy(n, i, c).start()

        @pl.when(i == NY - 1)
        def _():
            out_own(n).start()

    def hop(number):
        for part in "kv":
            arrived(f"u{number}{part}", f"d{number}{part}")
            send(f"u{number + 1}{part}", f"d{number + 1}{part}", f"x{-number}{part}", f"x{number}{part}")

    def event_q():
        q_copies[1].wait_recv()
        q_copies[3].wait_recv()

    def event_q2():
        q_copies[2].wait_recv()

    def event_hop1():
        hop(1)
        for d in Q_THIRD:
            q_copies[d].start()
        arrived("x0k", "x0v")

    def event_hop2():
        hop(2)

    def event_hop3():
        arrived("u3k", "d3k", "u3v", "d3v")
        send("u4k", "d4v")

    def event_far():
        arrived("x-1k", "x-1v", "x1k", "x1v")
        for part in "kv":
            arrived(f"x-2{part}", f"x2{part}")
            send(f"pu3{part}", f"pd3{part}")

    def event_first():
        arrived("u4k", "d4v")
        for b in range(NZ):
            piece = kvb[b, pl.ds(2 * BLK, NY * PIECE)].astype(f32).reshape(NY, 2, PRE_ROWS, DH)
            count = NY * PRE_ROWS
            kvb[PROMPT, pl.ds(b * count, count)] = piece[:, 0].reshape(count, DH).astype(bf16)
            kvb[PROMPT, pl.ds(BLK + b * count, count)] = piece[:, 1].reshape(count, DH).astype(bf16)
        flags[0, 0] = functools.reduce(
            jnp.maximum, [kvb[b, pl.ds(OWN_ROWS - 16, 16)].astype(f32) for b in range(NZ)])
        flag_copy(0).start()

    def event_last_hop():
        arrived("pu3k", "pd3k")
        send("pu4k")
        arrived("pu3v", "pd3v")
        send("pd4v")

    def event_second():
        arrived("pu4k", "pd4v")

    DIAG, ONE, PREFIX, TWO, NONE = range(5)
    own1 = (jnp.where(z >= 7, TWO, jnp.where(z >= 1, ONE, NONE)), 0, zb(-1), zb(1))
    own2 = (jnp.where(z >= 6, TWO, jnp.where(z >= 2, ONE, NONE)), 0, zb(-2), zb(2))
    own3 = (jnp.where(z >= 5, TWO, jnp.where(z >= 3, ONE, NONE)), 0, zb(-3), zb(3))
    own4 = (jnp.where(z >= 4, ONE, NONE), 0, zb(4), 0)
    diag = (DIAG, 0, z, 0)
    par0 = (ONE, 1, z, 0)
    pre0 = (PREFIX, 0, PROMPT, 0)
    pairs = [(TWO, 1, zb(-k), zb(k)) for k in (1, 2, 3)]
    low_z = z < LOW
    early_1 = (jnp.where(low_z, TWO, NONE),) + pairs[0][1:]
    late_1 = (jnp.where(low_z, NONE, TWO),) + pairs[0][1:]
    early = [
        diag + (0, 1),
        par0 + (0, 1),
        own1 + (0, 1),
        diag + (1, 3),
        par0 + (1, 3),
        own1 + (1, 3),
        diag + (3, 4),
        par0 + (3, 4),
        own1 + (3, 4),
        own2 + (0, 4),
        own3 + (0, 2),
        own3 + (2, 4),
    ]
    first_part = [own4, pre0]
    middle = [early_1 + (0, 2), early_1 + (2, 4)]
    second_part = [late_1, pairs[1], pairs[2], (ONE, 1, zb(4), 0)]
    begin_first = len(early)
    begin_middle = begin_first + NY * len(first_part)
    begin_second = begin_middle + len(middle)
    early = early + [(NONE, 0, 0, 0, 0, 0)] * (begin_middle - begin_first) + middle
    events = {1: event_hop1, 3: event_q, 6: event_q2, 5: event_hop2, 9: event_hop3, 11: event_far,
              begin_first: event_first, begin_middle: event_last_hop,
              begin_second + len(second_part) - 1: event_second}
    steps = {begin_second + k: r for k, r in ((0, 0), (3, 1), (6, 2), (9, 3), (12, 4))}

    def phase(n, carry):
        for at, event in events.items():
            pl.when(n == at)(event)
        for at, r in steps.items():
            pl.when(n == at)(functools.partial(flag_step, r))
        in_second = n >= begin_second
        in_first = jnp.logical_and(n >= begin_first, n < begin_middle)
        turn = jnp.where(in_second, (n - begin_second) // len(second_part), (n - begin_first) // len(first_part))
        step = jnp.where(in_second, (n - begin_second) % len(second_part), (n - begin_first) % len(first_part))

        def pick(column):
            value = jnp.int32(0)
            for k, row in enumerate(early):
                if k < begin_first or k >= begin_middle:
                    value = jnp.where(n == k, row[column], value)
            for k, row in enumerate(first_part):
                value = jnp.where(jnp.logical_and(in_first, step == k), row[column], value)
            for k, row in enumerate(second_part):
                value = jnp.where(jnp.logical_and(in_second, step == k), row[column], value)
            return value

        op, kind, b0, b1 = pick(0), pick(1), pick(2), pick(3)
        low = turn + 1
        high = turn + 2
        for k, row in enumerate(early):
            if begin_first <= k < begin_middle:
                continue
            low = jnp.where(n == k, row[4], low)
            high = jnp.where(n == k, row[5], high)

        def one(j, inner):
            c = chunk(lax.rem(j, NY))
            pl.when(op <= PREFIX)(lambda: single(c, kind, b0, op == DIAG))
            pl.when(op == TWO)(lambda: double(c, kind, [b0, b1]))

            @pl.when(op == PREFIX)
            def _():
                finish(0, turn, c, acc[c], tot[c])

            return inner

        lax.fori_loop(low, high, one, 0)

        @pl.when(jnp.logical_and(in_second, step == len(second_part) - 1))
        def _():
            c = chunk(lax.rem(turn + 1, NY))
            finish(1, turn, c, acc[c] + acc[NY + c], tot[c] + tot[NY + c])

        return carry

    lax.fori_loop(0, begin_second + NY * len(second_part), phase, 0)

    for n in range(2):
        for i in range(NY - 1):
            out_copy(n, i, chunk(i + 1)).wait()
        out_own(n).wait()
    for c in kv_copies + list(q_copies.values()) + list(ring.values()):
        c.wait_send()
    for r in range(len(rounds)):
        flag_copy(r).wait_send()


def fused(distance, lengths, q, k, v, pk, pv):
    vmem = pl.BlockSpec(memory_space=VMEM)
    out = jax.ShapeDtypeStruct((1, ROWS, QH * DH), bf16)
    dma = pltpu.SemaphoreType.DMA
    return pl.pallas_call(
        functools.partial(fused_kernel, distance),
        out_shape=(out, out, jax.ShapeDtypeStruct((16, DH), f32)),
        in_specs=[pl.BlockSpec(memory_space=pltpu.SMEM)] + [pl.BlockSpec(memory_space=pl.ANY)] * 5,
        out_specs=(pl.BlockSpec(memory_space=pl.ANY), pl.BlockSpec(memory_space=pl.ANY), vmem),
        scratch_shapes=[
            VMEM((PIECE, KVH * DH), bf16),
            VMEM((2, PRE_ROWS, KVH * DH), bf16),
            VMEM((ROWS, QH * DH), bf16),
            VMEM((ROWS, KVH * DH), bf16),
            VMEM((NY, ROWS, G * DH), bf16),
            VMEM((2 * NZ + 1, OWN_ROWS, DH), bf16),
            VMEM((2 * NY, STACK, DH), f32),
            VMEM((2 * NY, STACK, DH), f32),
            VMEM((NY, ROWS, G * DH), bf16),
            VMEM((NY, ROWS, G * DH), bf16),
            VMEM((2, 5, 16, DH), f32),
            dma((8,)),
            dma((NY - 1, 4)),
            dma((NY - 1, 4)),
            dma((30,)),
            dma((30,)),
            dma((2,)),
            dma((2, NY - 1)),
            dma((2, NY - 1)),
            dma((5,)),
            dma((5,)),
        ],
        compiler_params=pltpu.CompilerParams(
            collective_id=distance, has_side_effects=True, vmem_limit_bytes=56 << 20),
        name=f"fused_{distance}",
    )(lengths, q, k, v, pk, pv)


def settle_kernel(first, second, out1, out2):
    out1[...] = first[...]
    out2[...] = second[...]


def settle(first, second):
    block = pl.BlockSpec((1, ROWS // 4, QH * DH), lambda i: (0, i, 0))
    out = jax.ShapeDtypeStruct(first.shape, first.dtype)
    return pl.pallas_call(
        settle_kernel,
        out_shape=(out, out),
        grid=(4,),
        in_specs=[block, block],
        out_specs=(block, block),
        name="settle",
    )(first, second)


def local(queries, keys, values, prefix_keys, prefix_values, lengths, partner):
    branches = [functools.partial(fused, d) for d in range(1, 8)]
    first, second, level = lax.switch(
        partner[0] - 1, branches, lengths, queries[0], keys[0], values[0], prefix_keys, prefix_values)
    safe = jnp.max(level[:8]) * jnp.max(level[8:]) * (1.04 * SCALE2 * SCALE2) < SAFE * SAFE
    def redo(state):
        return (jnp.bool_(True),) + general(
            queries, keys, values, prefix_keys, prefix_values, lengths, partner)

    state = lax.while_loop(lambda state: jnp.logical_not(state[0]), redo, (safe, first, second))
    return settle(state[1], state[2])


def solution(mesh):
    in_specs = (
        P("pair", "section", None),
        P("pair", "section", None),
        P("pair", "section", None),
        P("section", None),
        P("section", None),
        P(),
        P(),
    )
    out_specs = (P("pair", "section", None), P("pair", "section", None))
    return jax.shard_map(local, mesh=mesh, in_specs=in_specs, out_specs=out_specs, check_vma=False)
```

```python
import functools

import jax
import jax.numpy as jnp
from jax import lax
from jax.experimental import pallas as pl
from jax.experimental.pallas import tpu as pltpu
from jax.sharding import PartitionSpec as P

QH = 32
KVH = 4
DH = 128
G = QH // KVH
NY = 4
NZ = 8
ROWS = 128
BLK = NY * ROWS
PRE_ROWS = 8
PIECE = 2 * PRE_ROWS
OWN_ROWS = 2 * BLK + NY * PIECE + 16
STACK = G * ROWS
SCALE2 = DH ** -0.5 * 1.4426950408889634
SAFE = 100.0
NEGATIVE = -1e30
NT = (((1,), (1,)), ((), ()))
f32 = jnp.float32
bf16 = jnp.bfloat16
VMEM = pltpu.VMEM
MESH = pl.DeviceIdType.MESH

def careful_kernel(sc, q, k, v, first, second, top, weight, mixed):
    block = pl.program_id(1)
    span = k.shape[0]
    prompt, length = PRE_ROWS * NY * NZ, ROWS * NY * NZ
    split = (prompt + length) // span

    @pl.when(block == 0)
    def _():
        top[...] = jnp.full_like(top, NEGATIVE)
        weight[...] = jnp.zeros_like(weight)
        mixed[...] = jnp.zeros_like(mixed)

    place = lax.broadcasted_iota(jnp.int32, (ROWS, span), 1) + (block * span - prompt)
    row = lax.broadcasted_iota(jnp.int32, (ROWS, span), 0) + sc[0] * ROWS
    limit = jnp.where(block < split, row + 1, length + sc[2])
    allowed = place < limit
    s = lax.dot_general(q[...], k[...], NT, preferred_element_type=f32)
    s = jnp.where(allowed, s, NEGATIVE)
    now = jnp.maximum(top[...], jnp.max(s, axis=1, keepdims=True))
    fade = jnp.exp2((top[...] - now) * SCALE2)
    p = jnp.where(allowed, jnp.exp2((s - now[:, :1]) * SCALE2), 0.0)
    top[...] = now
    weight[...] = weight[...] * fade + jnp.sum(p, axis=1, keepdims=True)
    mixed[...] = mixed[...] * fade + jnp.dot(p.astype(bf16), v[...], preferred_element_type=f32)
    place_row = lax.broadcasted_iota(jnp.int32, (ROWS, DH), 0) + sc[0] * ROWS

    def result():
        return jnp.where(place_row < sc[1], mixed[...] / weight[...], 0.0).astype(bf16)

    @pl.when(block == split - 1)
    def _():
        first[...] = result()

    @pl.when(block == split + length // span - 1)
    def _():
        second[...] = result()


def ring_gather(block, axis):
    size = lax.axis_size(axis)
    me = lax.axis_index(axis)
    route = [(i, (i + 1) % size) for i in range(size)]

    def step(i, carry):
        moving, held = carry
        owner = lax.rem(me - i + size, size)
        held = lax.dynamic_update_index_in_dim(held, moving, owner, 0)
        return lax.ppermute(moving, axis, route), held

    return lax.fori_loop(0, size, step, (block, jnp.zeros((size,) + block.shape, block.dtype)))[1]


def general(queries, keys, values, prefix_keys, prefix_values, lengths, partner):
    slot = lax.axis_index("pair")
    section = lax.axis_index("section")
    mine = jnp.concatenate([prefix_keys, prefix_values, keys[0], values[0]], axis=0)
    pair = ring_gather(mine, "pair")
    theirs = lax.dynamic_index_in_dim(pair, partner[slot], 0, keepdims=False)
    every = ring_gather(jnp.concatenate([mine, theirs[2 * PRE_ROWS:]], axis=0), "section")

    def stream(which):
        def rows_of(begin, count):
            return every[:, begin:begin + count].reshape(-1, KVH * DH)

        begin = 2 * PRE_ROWS + which * ROWS
        return jnp.concatenate([
            rows_of(which * PRE_ROWS, PRE_ROWS), rows_of(begin, ROWS), rows_of(begin + 2 * ROWS, ROWS)], axis=0)

    span = PRE_ROWS * NY * NZ
    blocks = (span + 2 * ROWS * NY * NZ) // span
    sc = jnp.stack([section, lengths[slot], lengths[partner[slot]]]).astype(jnp.int32)
    head = pl.BlockSpec((ROWS, DH), lambda h, b: (0, h))
    group = pl.BlockSpec((span, DH), lambda h, b: (b, h // G))
    out = jax.ShapeDtypeStruct((ROWS, QH * DH), bf16)
    first, second = pl.pallas_call(
        careful_kernel,
        out_shape=(out, out),
        grid=(QH, blocks),
        in_specs=[pl.BlockSpec(memory_space=pltpu.SMEM), head, group, group],
        out_specs=(head, head),
        scratch_shapes=[VMEM((ROWS, DH), f32)] * 3,
        name="careful",
    )(sc, queries[0], stream(0), stream(1))
    return first[None], second[None]


Q_FIRST = (1, 3)
Q_SECOND = ()
Q_THIRD = (2,)
LOW = 4
PROMPT = 2 * NZ


def at_section(z, y):
    return {"section": z * NY + y}


def fused_kernel(distance, lengths, q_ref, k_ref, v_ref, pk_ref, pv_ref, out1, out2, level,
                 pre, pre_in, q_in, k_in, qh, kvb, acc, tot, st1, st2, flags,
                 local_sem, a2a_send, a2a_recv, ring_send, ring_recv, out_local, out_send, out_recv,
                 flag_send, flag_recv):
    slot = lax.axis_index("pair")
    section = lax.axis_index("section")
    z = section // NY
    y = section % NY
    up = lax.rem(z + 1, NZ)
    down = lax.rem(z + NZ - 1, NZ)
    other = {"pair": slot ^ distance}
    own_length = lengths[slot]
    partner_length = lengths[slot ^ distance]

    def zb(step):
        return lax.rem(z + step + NZ, NZ)

    barrier = pltpu.get_barrier_semaphore()
    targets = [at_section(z, lax.rem(y + d, NY)) for d in range(1, NY)]
    targets += [at_section(t, y) for t in (up, down)]
    targets += [{"pair": slot ^ d} for d in sorted({1, 2, 4, distance})]
    for target in targets:
        pl.semaphore_signal(barrier, inc=1, device_id=target, device_id_type=MESH)
    staged = [pltpu.make_async_copy(src, dst, local_sem.at[4 + i]) for i, (src, dst) in enumerate(
        ((pk_ref, pre_in.at[0]), (pv_ref, pre_in.at[1]), (k_ref, k_in), (q_ref, q_in)))]
    for c in staged:
        c.start()
    staged[0].wait()
    staged[1].wait()
    pre[...] = jnp.concatenate([pre_in[0].astype(f32), pre_in[1].astype(f32)], axis=0).astype(bf16)
    pl.semaphore_wait(barrier, len(targets))

    def heads(ref, width, head):
        return ref.at[:, pl.ds(pl.multiple_of(head * width, 128), width)]

    def places(head):
        return [
            (heads(k_ref, DH, head), kvb.at[z, pl.ds(y * ROWS, ROWS)]),
            (heads(v_ref, DH, head), kvb.at[z, pl.ds(BLK + y * ROWS, ROWS)]),
            (heads(pre, DH, head), kvb.at[z, pl.ds(2 * BLK + y * PIECE, PIECE)]),
            (heads(q_ref, G * DH, head), qh.at[y]),
        ]

    def start_q_first():
        for d in Q_FIRST:
            q_copies[d].start()

    def start_q_second():
        for d in Q_SECOND:
            q_copies[d].start()

    kv_copies = []
    q_copies = {}
    for d in (1, 3, 2):
        head = lax.rem(y + d, NY)
        for i, (src, dst) in enumerate(places(head)):
            copy = pltpu.make_async_remote_copy(
                src_ref=src, dst_ref=dst, send_sem=a2a_send.at[d - 1, i], recv_sem=a2a_recv.at[d - 1, i],
                device_id=at_section(z, head), device_id_type=MESH)
            if i < 3:
                kv_copies.append(copy)
            else:
                q_copies[d] = copy
    locals_ = [pltpu.make_async_copy(src, dst, local_sem.at[i]) for i, (src, dst) in enumerate(places(y))]
    for c in kv_copies:
        c.start()
    for c in locals_:
        c.start()
    start_q_first()

    ring = {}
    keys_part = pl.ds(0, BLK)
    own_values = pl.ds(BLK, OWN_ROWS - BLK)
    par_values = pl.ds(BLK, BLK)
    to_up = at_section(up, y)
    to_down = at_section(down, y)
    routes = []
    for step in range(3):
        for part, rows in (("k", keys_part), ("v", own_values)):
            routes.append((f"u{step + 1}{part}", zb(-step), rows, to_up))
            routes.append((f"d{step + 1}{part}", zb(step), rows, to_down))
    for step in (0, -1, 1, -2, 2):
        for part, rows in (("k", keys_part), ("v", par_values)):
            routes.append((f"x{step}{part}", zb(step), rows, other))
    for part, rows in (("k", keys_part), ("v", par_values)):
        routes.append((f"pu3{part}", NZ + zb(-2), rows, to_up))
        routes.append((f"pd3{part}", NZ + zb(2), rows, to_down))
    routes.append(("u4k", zb(-3), keys_part, to_up))
    routes.append(("d4v", zb(3), own_values, to_down))
    routes.append(("pu4k", NZ + zb(-3), keys_part, to_up))
    routes.append(("pd4v", NZ + zb(3), par_values, to_down))
    for index, (name, block, rows, target) in enumerate(routes):
        to_block = NZ + block if name[0] == "x" else block
        ring[name] = pltpu.make_async_remote_copy(
            src_ref=kvb.at[block, rows], dst_ref=kvb.at[to_block, rows],
            send_sem=ring_send.at[index], recv_sem=ring_recv.at[index],
            device_id=target, device_id_type=MESH)

    def send(*which):
        for name in which:
            ring[name].start()

    def arrived(*which):
        for name in which:
            ring[name].wait_recv()

    rounds = [at_section(z, y ^ 1), at_section(z, y ^ 2),
              {"pair": slot ^ 1}, {"pair": slot ^ 2}, {"pair": slot ^ 4}]

    def flag_copy(r):
        return pltpu.make_async_remote_copy(
            src_ref=flags.at[0, r], dst_ref=flags.at[1, r], send_sem=flag_send.at[r], recv_sem=flag_recv.at[r],
            device_id=rounds[r], device_id_type=MESH)

    def flag_step(r):
        flag_copy(r).wait_recv()
        both = jnp.maximum(flags[0, r], flags[1, r])
        if r + 1 < len(rounds):
            flags[0, r + 1] = both
            flag_copy(r + 1).start()
        else:
            level[...] = both

    def squares(x):
        x = x.astype(f32)
        x = (x * x).astype(bf16)
        sums = jnp.dot(x, jnp.ones((DH, DH), bf16), preferred_element_type=f32)
        return functools.reduce(jnp.maximum, [sums[i:i + 8] for i in range(0, sums.shape[0], 8)])

    def q_head(h, top):
        return jnp.maximum(top, squares(q_in[:, pl.ds(pl.multiple_of(h * DH, DH), DH)]))

    staged[3].wait()
    q_top = lax.fori_loop(0, QH, q_head, jnp.zeros((8, DH), f32))
    staged[2].wait()
    k_top = jnp.zeros((8, DH), f32)
    for h in range(KVH):
        k_top = jnp.maximum(k_top, squares(k_in[:, h * DH:(h + 1) * DH]))
        k_top = jnp.maximum(k_top, squares(pre[:, h * DH:(h + 1) * DH])[:8])
    kvb[z, pl.ds(OWN_ROWS - 16, 16)] = jnp.concatenate([q_top, k_top], axis=0).astype(bf16)

    def clear(i, carry):
        acc[i] = jnp.zeros((STACK, DH), f32)
        tot[i] = jnp.zeros((STACK, DH), f32)
        return carry

    lax.fori_loop(0, 2 * NY, clear, 0)
    spare = jnp.zeros((BLK - NZ * NY * PRE_ROWS, DH), bf16)
    for begin in (NZ * NY * PRE_ROWS, BLK + NZ * NY * PRE_ROWS):
        kvb[PROMPT, pl.ds(begin, BLK - NZ * NY * PRE_ROWS)] = spare
    for c in locals_[:3]:
        c.wait()
    for c in kv_copies:
        c.wait_recv()
    send("u1k", "d1k", "x0k", "u1v", "d1v", "x0v")
    start_q_second()

    locals_[3].wait()

    def kv(b):
        return kvb[b, pl.ds(0, BLK)], kvb[b, pl.ds(BLK, BLK)]

    def lanes(p):
        return sum(p[:, i * DH:(i + 1) * DH] for i in range(p.shape[1] // DH))

    def unit(c, kind, parts):
        q = jnp.concatenate([qh[c, :, pl.ds(g * DH, DH)] for g in range(G)], axis=0)
        a = None
        t = None
        for keys, values, mask in parts:
            s = lax.dot_general(q, keys, NT, preferred_element_type=f32)
            p = jnp.exp2(s * SCALE2)
            if mask is not None:
                p = jnp.where(mask, p.reshape(G, ROWS, p.shape[1]), 0.0).reshape(p.shape)
            one = lanes(p)
            mixed = jnp.dot(p.astype(bf16), values, preferred_element_type=f32)
            a = mixed if a is None else a + mixed
            t = one if t is None else t + one
        acc[kind * NY + c] += a
        tot[kind * NY + c] += t

    def chunk(i):
        return lax.rem(y + (i ^ (i >> 1)), NY)

    def single(c, kind, b, causal):
        row = lax.broadcasted_iota(jnp.int32, (1, ROWS, 1), 1) + (c * ROWS + 1)
        limit = jnp.where(kind == 1, partner_length - b * BLK, jnp.where(b == PROMPT, NZ * NY * PRE_ROWS, BLK))
        limit = jnp.where(causal, row, limit)
        mask = lax.broadcasted_iota(jnp.int32, (1, ROWS, BLK), 2) < limit
        unit(c, kind, [kv(kind * NZ + b) + (mask,)])

    def double(c, kind, blocks):
        parts = []
        for b in blocks:
            limit = jnp.where(kind == 1, partner_length - b * BLK, BLK)
            mask = lax.broadcasted_iota(jnp.int32, (1, 1, BLK), 2) < limit
            parts.append(kv(kind * NZ + b) + (mask,))
        unit(c, kind, parts)

    mine = pl.ds(pl.multiple_of(y * G * DH, DH), G * DH)

    def out_copy(n, i, c):
        st, out = ((st1, out1), (st2, out2))[n]
        return pltpu.make_async_remote_copy(
            src_ref=st.at[c], dst_ref=out.at[0, :, mine], send_sem=out_send.at[n, i], recv_sem=out_recv.at[n, i],
            device_id=at_section(z, c), device_id_type=MESH)

    def out_own(n):
        st, out = ((st1, out1), (st2, out2))[n]
        return pltpu.make_async_copy(st.at[y], out.at[0, :, mine], out_local.at[n])

    def finish(n, i, c, a, t):
        st = (st1, st2)[n]
        row = lax.broadcasted_iota(jnp.int32, (1, ROWS, 1), 1) + (z * BLK + c * ROWS)
        mixed = (a * (1.0 / jnp.sum(t, axis=1, keepdims=True))).reshape(G, ROWS, DH)
        mixed = jnp.where(row < own_length, mixed, 0.0).astype(bf16)
        for g in range(G):
            st[c, :, pl.ds(g * DH, DH)] = mixed[g]

        @pl.when(i < NY - 1)
        def _():
            out_copy(n, i, c).start()

        @pl.when(i == NY - 1)
        def _():
            out_own(n).start()

    def hop(number):
        for part in "kv":
            arrived(f"u{number}{part}", f"d{number}{part}")
            send(f"u{number + 1}{part}", f"d{number + 1}{part}", f"x{-number}{part}", f"x{number}{part}")

    def event_q():
        q_copies[1].wait_recv()
        q_copies[3].wait_recv()

    def event_q2():
        q_copies[2].wait_recv()

    def event_hop1():
        hop(1)
        for d in Q_THIRD:
            q_copies[d].start()
        arrived("x0k", "x0v")

    def event_hop2():
        hop(2)

    def event_hop3():
        arrived("u3k", "d3k", "u3v", "d3v")
        send("u4k", "d4v")

    def event_far():
        arrived("x-1k", "x-1v", "x1k", "x1v")
        for part in "kv":
            arrived(f"x-2{part}", f"x2{part}")
            send(f"pu3{part}", f"pd3{part}")

    def event_first():
        arrived("u4k", "d4v")
        for b in range(NZ):
            piece = kvb[b, pl.ds(2 * BLK, NY * PIECE)].astype(f32).reshape(NY, 2, PRE_ROWS, DH)
            count = NY * PRE_ROWS
            kvb[PROMPT, pl.ds(b * count, count)] = piece[:, 0].reshape(count, DH).astype(bf16)
            kvb[PROMPT, pl.ds(BLK + b * count, count)] = piece[:, 1].reshape(count, DH).astype(bf16)
        flags[0, 0] = functools.reduce(
            jnp.maximum, [kvb[b, pl.ds(OWN_ROWS - 16, 16)].astype(f32) for b in range(NZ)])
        flag_copy(0).start()

    def event_last_hop():
        arrived("pu3k", "pd3k")
        send("pu4k")
        arrived("pu3v", "pd3v")
        send("pd4v")

    def event_second():
        arrived("pu4k", "pd4v")

    DIAG, ONE, PREFIX, TWO, NONE = range(5)
    own1 = (jnp.where(z >= 7, TWO, jnp.where(z >= 1, ONE, NONE)), 0, zb(-1), zb(1))
    own2 = (jnp.where(z >= 6, TWO, jnp.where(z >= 2, ONE, NONE)), 0, zb(-2), zb(2))
    own3 = (jnp.where(z >= 5, TWO, jnp.where(z >= 3, ONE, NONE)), 0, zb(-3), zb(3))
    own4 = (jnp.where(z >= 4, ONE, NONE), 0, zb(4), 0)
    diag = (DIAG, 0, z, 0)
    par0 = (ONE, 1, z, 0)
    pre0 = (PREFIX, 0, PROMPT, 0)
    pairs = [(TWO, 1, zb(-k), zb(k)) for k in (1, 2, 3)]
    low_z = z < LOW
    early_1 = (jnp.where(low_z, TWO, NONE),) + pairs[0][1:]
    late_1 = (jnp.where(low_z, NONE, TWO),) + pairs[0][1:]
    early = [
        diag + (0, 1),
        par0 + (0, 1),
        own1 + (0, 1),
        diag + (1, 3),
        par0 + (1, 3),
        own1 + (1, 3),
        diag + (3, 4),
        par0 + (3, 4),
        own1 + (3, 4),
        own2 + (0, 4),
        own3 + (0, 2),
        own3 + (2, 4),
    ]
    first_part = [own4, pre0]
    middle = [early_1 + (0, 2), early_1 + (2, 4)]
    second_part = [late_1, pairs[1], pairs[2], (ONE, 1, zb(4), 0)]
    begin_first = len(early)
    begin_middle = begin_first + NY * len(first_part)
    begin_second = begin_middle + len(middle)
    early = early + [(NONE, 0, 0, 0, 0, 0)] * (begin_middle - begin_first) + middle
    events = {1: event_hop1, 3: event_q, 6: event_q2, 5: event_hop2, 9: event_hop3, 11: event_far,
              begin_first: event_first, begin_middle: event_last_hop,
              begin_second + len(second_part) - 1: event_second}
    steps = {begin_second + k: r for k, r in ((0, 0), (3, 1), (6, 2), (9, 3), (12, 4))}

    def phase(n, carry):
        for at, event in events.items():
            pl.when(n == at)(event)
        for at, r in steps.items():
            pl.when(n == at)(functools.partial(flag_step, r))
        in_second = n >= begin_second
        in_first = jnp.logical_and(n >= begin_first, n < begin_middle)
        turn = jnp.where(in_second, (n - begin_second) // len(second_part), (n - begin_first) // len(first_part))
        step = jnp.where(in_second, (n - begin_second) % len(second_part), (n - begin_first) % len(first_part))

        def pick(column):
            value = jnp.int32(0)
            for k, row in enumerate(early):
                if k < begin_first or k >= begin_middle:
                    value = jnp.where(n == k, row[column], value)
            for k, row in enumerate(first_part):
                value = jnp.where(jnp.logical_and(in_first, step == k), row[column], value)
            for k, row in enumerate(second_part):
                value = jnp.where(jnp.logical_and(in_second, step == k), row[column], value)
            return value

        op, kind, b0, b1 = pick(0), pick(1), pick(2), pick(3)
        low = turn + 1
        high = turn + 2
        for k, row in enumerate(early):
            if begin_first <= k < begin_middle:
                continue
            low = jnp.where(n == k, row[4], low)
            high = jnp.where(n == k, row[5], high)

        def one(j, inner):
            c = chunk(lax.rem(j, NY))
            pl.when(op <= PREFIX)(lambda: single(c, kind, b0, op == DIAG))
            pl.when(op == TWO)(lambda: double(c, kind, [b0, b1]))

            @pl.when(op == PREFIX)
            def _():
                finish(0, turn, c, acc[c], tot[c])

            return inner

        lax.fori_loop(low, high, one, 0)

        @pl.when(jnp.logical_and(in_second, step == len(second_part) - 1))
        def _():
            c = chunk(lax.rem(turn + 1, NY))
            finish(1, turn, c, acc[c] + acc[NY + c], tot[c] + tot[NY + c])

        return carry

    lax.fori_loop(0, begin_second + NY * len(second_part), phase, 0)

    for n in range(2):
        for i in range(NY - 1):
            out_copy(n, i, chunk(i + 1)).wait()
        out_own(n).wait()
    for c in kv_copies + list(q_copies.values()) + list(ring.values()):
        c.wait_send()
    for r in range(len(rounds)):
        flag_copy(r).wait_send()


def fused(distance, lengths, q, k, v, pk, pv):
    vmem = pl.BlockSpec(memory_space=VMEM)
    out = jax.ShapeDtypeStruct((1, ROWS, QH * DH), bf16)
    dma = pltpu.SemaphoreType.DMA
    return pl.pallas_call(
        functools.partial(fused_kernel, distance),
        out_shape=(out, out, jax.ShapeDtypeStruct((16, DH), f32)),
        in_specs=[pl.BlockSpec(memory_space=pltpu.SMEM)] + [pl.BlockSpec(memory_space=pl.ANY)] * 5,
        out_specs=(pl.BlockSpec(memory_space=pl.ANY), pl.BlockSpec(memory_space=pl.ANY), vmem),
        scratch_shapes=[
            VMEM((PIECE, KVH * DH), bf16),
            VMEM((2, PRE_ROWS, KVH * DH), bf16),
            VMEM((ROWS, QH * DH), bf16),
            VMEM((ROWS, KVH * DH), bf16),
            VMEM((NY, ROWS, G * DH), bf16),
            VMEM((2 * NZ + 1, OWN_ROWS, DH), bf16),
            VMEM((2 * NY, STACK, DH), f32),
            VMEM((2 * NY, STACK, DH), f32),
            VMEM((NY, ROWS, G * DH), bf16),
            VMEM((NY, ROWS, G * DH), bf16),
            VMEM((2, 5, 16, DH), f32),
            dma((8,)),
            dma((NY - 1, 4)),
            dma((NY - 1, 4)),
            dma((30,)),
            dma((30,)),
            dma((2,)),
            dma((2, NY - 1)),
            dma((2, NY - 1)),
            dma((5,)),
            dma((5,)),
        ],
        compiler_params=pltpu.CompilerParams(
            collective_id=distance, has_side_effects=True, vmem_limit_bytes=56 << 20),
        name=f"fused_{distance}",
    )(lengths, q, k, v, pk, pv)


def settle_kernel(first, second, out1, out2):
    out1[...] = first[...]
    out2[...] = second[...]


def settle(first, second):
    block = pl.BlockSpec((1, ROWS // 4, QH * DH), lambda i: (0, i, 0))
    out = jax.ShapeDtypeStruct(first.shape, first.dtype)
    return pl.pallas_call(
        settle_kernel,
        out_shape=(out, out),
        grid=(4,),
        in_specs=[block, block],
        out_specs=(block, block),
        name="settle",
    )(first, second)


def local(queries, keys, values, prefix_keys, prefix_values, lengths, partner):
    branches = [functools.partial(fused, d) for d in range(1, 8)]
    first, second, level = lax.switch(
        partner[0] - 1, branches, lengths, queries[0], keys[0], values[0], prefix_keys, prefix_values)
    safe = jnp.max(level[:8]) * jnp.max(level[8:]) * (1.04 * SCALE2 * SCALE2) < SAFE * SAFE
    def redo(state):
        return (jnp.bool_(True),) + general(
            queries, keys, values, prefix_keys, prefix_values, lengths, partner)

    state = lax.while_loop(lambda state: jnp.logical_not(state[0]), redo, (safe, first, second))
    return settle(state[1], state[2])


def solution(mesh):
    in_specs = (
        P("pair", "section", None),
        P("pair", "section", None),
        P("pair", "section", None),
        P("section", None),
        P("section", None),
        P(),
        P(),
    )
    out_specs = (P("pair", "section", None), P("pair", "section", None))
    return jax.shard_map(local, mesh=mesh, in_specs=in_specs, out_specs=out_specs, check_vma=False)
```
